32 devices in a mesh: dp: 8 (over z, x), blk: 4 (over y, core).
Axes of the slice: x: 2, y: 2, z: 4, core: 2. Of those that a mesh axis runs over, the one named last changes fastest.
Arguments:
- hidden_pre: bfloat16 [1536, 24576], P('dp', 'blk'), may hold values from -6 to 6
- out_grad: bfloat16 [1536, 6144], P('dp', 'blk'), may hold values from -6 to 6
- w_up_blocks: bfloat16 [1152, 128, 128], P('blk'), may hold values from -0.109375 to 0.109375
- up_index: int32 [1152, 2], P('blk'), may hold values from 0 to 47, as said below
- w_down_blocks: bfloat16 [1152, 128, 128], P('blk'), may hold values from -0.21875 to 0.21875
- down_index: int32 [1152, 2], P('blk'), may hold values from 0 to 47, as said below
Outputs:
- in_grad: bfloat16 [1536, 6144], P('dp', 'blk')
- w_down_grad: float32 [147456, 128], P(('blk', 'dp'))
The draws below stay inside these ranges and needn't reach their ends.
Inputs may be any that keep to these rules, and one draw needn't show every extreme that they name: `up_index`: each run of 288 rows that starts at a multiple of 288 belongs to one shard and lists distinct pairs (r, c) with r below 48 and c below 48; every shard holds the pair (47, 47). `down_index`: each run of 288 rows that starts at a multiple of 288 belongs to one shard and lists distinct pairs (r, c) with r below 48 and c below 48; every shard holds the pair (47, 47).
All inputs are finite; a program needn't handle non-finite values.
Results may differ from the reference program's by a relative error of at most 0.014.
Values may be sent and summed in bfloat16 or wider, within the bound.
A program may use at most 192 MiB of HBM per device.

```python
import jax
import jax.numpy as jnp
from jax import lax

D = 6144
FF = 24576
BLOCK = 128
DBLK = 48
FBLK = 48
NB = 288
BLOCKS = 1152
TOKENS = 1536


def block_pattern(key):
    shards = BLOCKS // NB
    cells = DBLK * FBLK

    def one_shard(shard_id):
        shard_key = jax.random.fold_in(key, shard_id)
        perm_key, score_key = jax.random.split(shard_key)
        order = jax.random.permutation(perm_key, DBLK)
        factor = jnp.where(order < DBLK // 4, 4, 1).astype(jnp.int32)
        cell_ids = jnp.arange(cells, dtype=jnp.int32)
        scores = jax.random.randint(score_key, (cells,), 0, 65536, dtype=jnp.int32) * factor[cell_ids // FBLK] * cells + cell_ids
        scores = jnp.where(cell_ids == cells - 1, 262144 * cells, scores).astype(jnp.int32)
        _, chosen = lax.top_k(scores, NB)
        chosen = chosen.astype(jnp.int32)
        return jnp.stack([chosen // FBLK, chosen % FBLK], axis=1)
    return jax.vmap(one_shard)(jnp.arange(shards, dtype=jnp.int32)).reshape(BLOCKS, 2).astype(jnp.int32)


def draw_up_index(key, part):
    key = jax.random.fold_in(key, 11)
    return block_pattern(key)


def draw_down_index(key, part):
    key = jax.random.fold_in(key, 23)
    return block_pattern(key)


def block_levels(stream_key, dims, cuts, least, top_value):
    factor_of = 1.0
    for position, blocks in cuts:
        heights = jax.random.uniform(jax.random.fold_in(jax.random.fold_in(stream_key, 6), position), (blocks,), jnp.float32, least / len(cuts), top_value / len(cuts))
        factor_of = factor_of * jnp.repeat(jnp.exp(heights), dims[position] // blocks).reshape((-1,) + (1,) * (len(dims) - 1 - position))
    return factor_of


def bell_draw(stream_key, extent, width, limit, pieces=(), kind=jnp.bfloat16):
    level = block_levels(stream_key, extent, pieces, -0.22, 0.18) if pieces else 1.0
    values = jax.random.normal(stream_key, extent, jnp.float32) * width * level
    return jnp.minimum(jnp.maximum(values, -limit), limit).astype(kind)


def setup_inputs(seed: int = 0) -> dict:
    splits = jax.random.split(jax.random.key(seed), 7)
    return {
        "hidden_pre": bell_draw(splits[0], (TOKENS, FF), 1.0, 6.0, ((0, 8), (1, 4))),
        "out_grad": bell_draw(splits[1], (TOKENS, D), 1.0, 6.0, ((0, 8), (1, 4))),
        "w_up_blocks": bell_draw(splits[2], (BLOCKS, BLOCK, BLOCK), (FF // 8) ** -0.5, 0.109375, ((0, 4),)),
        "up_index": draw_up_index(jax.random.fold_in(splits[6], 71), 0),
        "w_down_blocks": bell_draw(splits[4], (BLOCKS, BLOCK, BLOCK), (D // 8) ** -0.5, 0.21875, ((0, 4),)),
        "down_index": draw_down_index(jax.random.fold_in(splits[6], 71), 0),
    }


inv_root_two = 0.7071067811865476
inv_root_twopi = 0.3989422804014327

def gelu_parts(pre_float):
    normal_cdf = 0.5 * (1.0 + lax.erf(pre_float * inv_root_two))
    gelu_slope = normal_cdf + pre_float * jnp.exp(-0.5 * pre_float * pre_float) * inv_root_twopi
    return (pre_float * normal_cdf, gelu_slope)

def reference(hidden_pre, out_grad, w_up_blocks, up_index, w_down_blocks, down_index):
    shards = BLOCKS // NB
    grad_scale = jnp.float32(1.0) / jnp.sqrt(jnp.float32(TOKENS))
    grad_cube = out_grad.reshape(TOKENS, DBLK, BLOCK)
    feat_ids = jnp.arange(DBLK, dtype=jnp.int32)
    hid_ids = jnp.arange(FBLK, dtype=jnp.int32)

    def one_shard(total_sum, shard_id):
        start_col = (shard_id * FBLK * BLOCK).astype(jnp.int32)
        start_blk = (shard_id * NB).astype(jnp.int32)
        pre_shard = lax.dynamic_slice_in_dim(hidden_pre, start_col, FBLK * BLOCK, 1).astype(jnp.float32)
        up_shard = lax.dynamic_slice_in_dim(w_up_blocks, start_blk, NB, 0).astype(jnp.float32)
        down_shard = lax.dynamic_slice_in_dim(w_down_blocks, start_blk, NB, 0).astype(jnp.float32)
        up_pairs = lax.dynamic_slice_in_dim(up_index, start_blk, NB, 0)
        down_pairs = lax.dynamic_slice_in_dim(down_index, start_blk, NB, 0)
        act_float, gelu_slope = gelu_parts(pre_shard)
        activation = act_float.astype(jnp.bfloat16)
        grad_panels = jnp.take(grad_cube, down_pairs[:, 0], axis=1).astype(jnp.float32)
        down_terms = jnp.einsum('tbj,bij->tbi', grad_panels, down_shard)
        down_pick = (down_pairs[:, 1][:, None] == hid_ids[None, :]).astype(jnp.float32)
        act_grad = jnp.einsum('tbi,bf->tfi', down_terms, down_pick).reshape(TOKENS, FBLK * BLOCK)
        pre_grad = (act_grad * gelu_slope).astype(jnp.bfloat16)
        pre_panels = jnp.take(pre_grad.reshape(TOKENS, FBLK, BLOCK), up_pairs[:, 1], axis=1).astype(jnp.float32)
        up_terms = jnp.einsum('tbi,bji->tbj', pre_panels, up_shard)
        up_pick = (up_pairs[:, 0][:, None] == feat_ids[None, :]).astype(jnp.float32)
        partial_sum = jnp.einsum('tbj,bd->tdj', up_terms, up_pick).reshape(TOKENS, D).astype(jnp.bfloat16)
        act_panels = jnp.take(activation.reshape(TOKENS, FBLK, BLOCK), down_pairs[:, 1], axis=1).astype(jnp.float32)
        weight_grad = jnp.einsum('tbi,tbj->bij', act_panels, grad_panels) * grad_scale
        return (total_sum + partial_sum.astype(jnp.float32), weight_grad)
    start_sum = jnp.zeros((TOKENS, D), jnp.float32)
    total_sum, weight_grads = lax.scan(one_shard, start_sum, jnp.arange(shards, dtype=jnp.int32))
    return (total_sum.astype(jnp.bfloat16), weight_grads.reshape(BLOCKS * BLOCK, BLOCK))
```

```python
import functools

import jax
import jax.numpy as jnp
from jax import lax
from jax.experimental import pallas as pl
from jax.experimental.pallas import tpu as pltpu
from jax.sharding import PartitionSpec as P

inv_root_two = 0.7071067811865476
inv_root_twopi = 0.3989422804014327
MESH = pl.DeviceIdType.MESH
VMEM_BYTES = 58 << 20
DEEP, WIDE = 4, 2


def contract_last(a, b):
    return lax.dot_general(
        a, b, (((1,), (1,)), ((), ())), preferred_element_type=jnp.float32
    )


def chunk_of(count, most):
    return max(n for n in range(1, most + 1) if count % n == 0)


def hidden_kernel(
    per_step, group, down_ref, up_ref, grad_ref, slope_ref, wd_ref, wu_ref, out_ref,
    hid_acc, pre, feat_acc,
):
    phase, step = pl.program_id(0), pl.program_id(1)
    last = pl.num_programs(1) - 1

    @pl.when((phase == 0) & (step == 0))
    def _():
        hid_acc[...] = jnp.zeros_like(hid_acc)
        feat_acc[...] = jnp.zeros_like(feat_acc)

    @pl.when(phase == 0)
    def _():
        @pl.loop(0, per_step // group)
        def _(g):
            first = step * per_step + g * group
            terms = [
                contract_last(grad_ref[down_ref[first + i, 0]], wd_ref[g * group + i])
                for i in range(group)
            ]
            for i in range(group):
                hid_acc[down_ref[first + i, 1]] += terms[i]

    @pl.when((phase == 0) & (step == last))
    def _():
        @pl.loop(0, pre.shape[0])
        def _(c):
            pre[c] = (hid_acc[c] * slope_ref[c]).astype(pre.dtype)

    @pl.when(phase == 1)
    def _():
        @pl.loop(0, per_step // group)
        def _(g):
            first = step * per_step + g * group
            terms = [
                contract_last(pre[up_ref[first + i, 1]], wu_ref[g * group + i])
                for i in range(group)
            ]
            for i in range(group):
                feat_acc[up_ref[first + i, 0]] += terms[i]

    @pl.when((phase == 1) & (step == last))
    def _():
        @pl.loop(0, feat_acc.shape[0])
        def _(r):
            out_ref[r] = feat_acc[r].astype(out_ref.dtype)


def hidden_call(down_index, up_index, grads, slope, w_down, w_up):
    feats, rows, side = grads.shape
    hids = slope.shape[0]
    count = w_down.shape[0]
    per_step = chunk_of(count, 24)
    group = chunk_of(per_step, 8)
    steps = count // per_step
    whole = lambda shape: pl.BlockSpec(shape, lambda p, s, *_: (0, 0, 0))
    return pl.pallas_call(
        functools.partial(hidden_kernel, per_step, group),
        grid_spec=pltpu.PrefetchScalarGridSpec(
            num_scalar_prefetch=2,
            grid=(2, steps),
            in_specs=[
                whole(grads.shape),
                whole(slope.shape),
                pl.BlockSpec(
                    (per_step, side, side),
                    lambda p, s, *_: (jnp.where(p == 0, s, steps - 1), 0, 0),
                ),
                pl.BlockSpec(
                    (per_step, side, side),
                    lambda p, s, *_: (jnp.where(p == 0, 0, s), 0, 0),
                ),
            ],
            out_specs=whole(grads.shape),
            scratch_shapes=[
                pltpu.VMEM((hids, rows, side), jnp.float32),
                pltpu.VMEM((hids, rows, side), jnp.bfloat16),
                pltpu.VMEM((feats, rows, side), jnp.float32),
            ],
        ),
        out_shape=jax.ShapeDtypeStruct(grads.shape, jnp.bfloat16),
        compiler_params=pltpu.CompilerParams(vmem_limit_bytes=VMEM_BYTES),
        cost_estimate=pl.CostEstimate(
            flops=4 * count * rows * side * side,
            bytes_accessed=4 * count * side * side,
            transcendentals=0,
        ),
        name="hidden_grads",
    )(down_index, up_index, grads, slope, w_down, w_up)


def weight_kernel(
    chunks, ahead, scale, hid_ids, feat_ids, act_ref, grad_ref, out_ref,
    x_out, x_in, up_in, dn_in, z_out, acc,
    x_send, x_recv, up_recv, dn_recv, z_send,
):
    blk = lax.axis_index("blk")
    dp = lax.axis_index("dp")
    z, x = dp // WIDE, dp % WIDE
    per = out_ref.shape[0]
    n = per // chunks
    items = DEEP * chunks

    def at(zz, xx):
        return (zz * WIDE + xx, blk)

    barrier = pltpu.get_barrier_semaphore()
    pl.semaphore_signal(barrier, inc=1, device_id=at(z, 1 - x), device_id_type=MESH)

    @pl.when(z > 0)
    def _():
        pl.semaphore_signal(barrier, inc=1, device_id=at(z - 1, x), device_id_type=MESH)

    @pl.when(z < DEEP - 1)
    def _():
        pl.semaphore_signal(barrier, inc=1, device_id=at(z + 1, x), device_id_type=MESH)

    peers = 1 + (z > 0).astype(jnp.int32) + (z < DEEP - 1).astype(jnp.int32)
    pl.semaphore_wait(barrier, peers)

    def place(t):
        half, r = t // (2 * chunks), t % (2 * chunks)
        c, low = r // 2, r % 2
        return jnp.where(low == 0, DEEP - 1 - half, half), c

    def product(k):
        return jnp.dot(
            act_ref[hid_ids[k]], grad_ref[feat_ids[k]], preferred_element_type=jnp.float32
        )

    def x_copy(t):
        return pltpu.make_async_remote_copy(
            src_ref=x_out.at[t], dst_ref=x_in.at[t], send_sem=x_send.at[t],
            recv_sem=x_recv.at[t], device_id=at(z, 1 - x), device_id_type=MESH,
        )

    def up_copy(t):
        return pltpu.make_async_remote_copy(
            src_ref=z_out.at[t], dst_ref=up_in.at[t], send_sem=z_send.at[t],
            recv_sem=up_recv.at[t], device_id=at(z + 1, x), device_id_type=MESH,
        )

    def dn_copy(t):
        return pltpu.make_async_remote_copy(
            src_ref=z_out.at[t], dst_ref=dn_in.at[t], send_sem=z_send.at[t],
            recv_sem=dn_recv.at[t], device_id=at(z - 1, x), device_id_type=MESH,
        )

    def send_x(t):
        zt, c = place(t)
        base = (zt * WIDE + 1 - x) * per + c * n
        for i in range(n):
            x_out[t, i] = product(base + i).astype(x_out.dtype)
        x_copy(t).start()

    def handle(t):
        zt, c = place(t)
        base = (zt * WIDE + x) * per + c * n
        for i in range(n):
            acc[i] = product(base + i)
        x_copy(t).wait_recv()
        acc[...] += x_in[t].astype(jnp.float32)

        @pl.when((z <= zt) & (z > 0))
        def _():
            up_copy(t).wait_recv()
            acc[...] += up_in[t].astype(jnp.float32)

        @pl.when((z >= zt) & (z < DEEP - 1))
        def _():
            dn_copy(t).wait_recv()
            acc[...] += dn_in[t].astype(jnp.float32)

        @pl.when(z == zt)
        def _():
            out_ref[pl.ds(c * n, n)] = acc[...] * scale

        @pl.when(z < zt)
        def _():
            z_out[t] = acc[...].astype(z_out.dtype)
            up_copy(t).start()

        @pl.when(z > zt)
        def _():
            z_out[t] = acc[...].astype(z_out.dtype)
            dn_copy(t).start()

    @pl.loop(0, ahead)
    def _(t):
        send_x(t)

    @pl.loop(0, items + DEEP - 1)
    def _(u):
        @pl.when(u + ahead < items)
        def _():
            x_copy(u).wait_send()
            send_x(u + ahead)

        @pl.loop(0, DEEP)
        def _(lag):
            t = u - lag
            safe = jnp.clip(t, 0, items - 1)
            zt, _ = place(safe)
            late = jnp.where(
                z < zt, z, jnp.where(z > zt, DEEP - 1 - z, jnp.maximum(z, DEEP - 1 - z))
            )

            @pl.when((t >= 0) & (t < items) & (late == lag))
            def _():
                handle(safe)

    @pl.loop(items - ahead, items)
    def _(t):
        x_copy(t).wait_send()

    @pl.loop(0, items)
    def _(t):
        zt, _ = place(t)

        @pl.when(z != zt)
        def _():
            up_copy(t).wait_send()


def weight_call(hid_ids, feat_ids, acts, grads, scale):
    hids, side, rows = acts.shape
    count = hid_ids.shape[0]
    per = count // (DEEP * WIDE)
    chunks = chunk_of(per, 4)
    n = per // chunks
    items = DEEP * chunks
    ahead = min(3, items)
    slots = pltpu.VMEM((items, n, side, side), jnp.bfloat16)
    sems = pltpu.SemaphoreType.DMA((items,))
    return pl.pallas_call(
        functools.partial(weight_kernel, chunks, ahead, scale),
        out_shape=jax.ShapeDtypeStruct((per, side, side), jnp.float32),
        in_specs=[pl.BlockSpec(memory_space=pltpu.SMEM)] * 2
        + [pl.BlockSpec(memory_space=pltpu.VMEM)] * 2,
        out_specs=pl.BlockSpec(memory_space=pltpu.VMEM),
        scratch_shapes=[slots] * 5
        + [pltpu.VMEM((n, side, side), jnp.float32)]
        + [sems] * 5,
        compiler_params=pltpu.CompilerParams(
            collective_id=0, has_side_effects=True, vmem_limit_bytes=VMEM_BYTES
        ),
        cost_estimate=pl.CostEstimate(
            flops=2 * count * rows * side * side,
            bytes_accessed=4 * count * side * side,
            transcendentals=0,
        ),
        name="weight_grads",
    )(hid_ids, feat_ids, acts, grads)


def local(hidden_pre, out_grad, w_up_blocks, up_index, w_down_blocks, down_index):
    rows, hid_width = hidden_pre.shape
    side = w_up_blocks.shape[1]
    hids = hid_width // side
    count = w_down_blocks.shape[0]
    dp_size = lax.axis_size("dp")
    scale = float((rows * dp_size) ** (-0.5))
    own = out_grad.reshape(rows, -1, side).transpose(1, 0, 2)
    grads = lax.all_gather(own, "blk", axis=0, tiled=True)
    feats = grads.shape[0]
    pre_float = hidden_pre.astype(jnp.float32)
    normal_cdf = 0.5 * (1.0 + lax.erf(pre_float * inv_root_two))
    slope = normal_cdf + pre_float * jnp.exp(-0.5 * pre_float * pre_float) * inv_root_twopi
    slope = slope.reshape(rows, hids, side).transpose(1, 0, 2)
    acts = (pre_float * normal_cdf).astype(jnp.bfloat16)
    acts = acts.reshape(rows, hids, side).transpose(1, 2, 0)
    partial_sum = hidden_call(down_index, up_index, grads, slope, w_down_blocks, w_up_blocks)
    summed = lax.psum_scatter(partial_sum, "blk", scatter_dimension=0, tiled=True)
    summed = summed.transpose(1, 0, 2).reshape(rows, -1)
    if dp_size == DEEP * WIDE and count % dp_size == 0:
        weight_out = weight_call(down_index[:, 1], down_index[:, 0], acts, grads, scale)
        weight_out = weight_out.reshape(-1, side)
    else:
        local_grad = jnp.einsum(
            "bit,btj->bij",
            jnp.take(acts, down_index[:, 1], axis=0),
            jnp.take(grads, down_index[:, 0], axis=0),
            preferred_element_type=jnp.float32,
        )
        weight_out = lax.psum_scatter(
            (local_grad * scale).reshape(-1, side), "dp", scatter_dimension=0, tiled=True
        )
    return (summed, weight_out)


def solution(mesh):
    placed = (
        P("dp", "blk"),
        P("dp", "blk"),
        P("blk", None, None),
        P("blk", None),
        P("blk", None, None),
        P("blk", None),
    )
    return jax.shard_map(
        local,
        mesh=mesh,
        in_specs=placed,
        out_specs=(P("dp", "blk"), P(("blk", "dp"), None)),
        check_vma=False,
    )
```

```python
import functools

import jax
import jax.numpy as jnp
from jax import lax
from jax.experimental import pallas as pl
from jax.experimental.pallas import tpu as pltpu
from jax.sharding import PartitionSpec as P

inv_root_two = 0.7071067811865476
inv_root_twopi = 0.3989422804014327
MESH = pl.DeviceIdType.MESH
VMEM_BYTES = 58 << 20
DEEP, WIDE = 4, 2


def contract_last(a, b):
    return lax.dot_general(
        a, b, (((1,), (1,)), ((), ())), preferred_element_type=jnp.float32
    )


def chunk_of(count, most):
    return max(n for n in range(1, most + 1) if count % n == 0)


def hidden_kernel(
    per_step, group, down_ref, up_ref, grad_ref, slope_ref, wd_ref, wu_ref, out_ref,
    hid_acc, pre, feat_acc,
):
    phase, step = pl.program_id(0), pl.program_id(1)
    last = pl.num_programs(1) - 1

    @pl.when((phase == 0) & (step == 0))
    def _():
        hid_acc[...] = jnp.zeros_like(hid_acc)
        feat_acc[...] = jnp.zeros_like(feat_acc)

    @pl.when(phase == 0)
    def _():
        @pl.loop(0, per_step // group)
        def _(g):
            first = step * per_step + g * group
            terms = [
                contract_last(grad_ref[down_ref[first + i, 0]], wd_ref[g * group + i])
                for i in range(group)
            ]
            for i in range(group):
                hid_acc[down_ref[first + i, 1]] += terms[i]

    @pl.when((phase == 0) & (step == last))
    def _():
        @pl.loop(0, pre.shape[0])
        def _(c):
            pre[c] = (hid_acc[c] * slope_ref[c]).astype(pre.dtype)

    @pl.when(phase == 1)
    def _():
        @pl.loop(0, per_step // group)
        def _(g):
            first = step * per_step + g * group
            terms = [
                contract_last(pre[up_ref[first + i, 1]], wu_ref[g * group + i])
                for i in range(group)
            ]
            for i in range(group):
                feat_acc[up_ref[first + i, 0]] += terms[i]

    @pl.when((phase == 1) & (step == last))
    def _():
        @pl.loop(0, feat_acc.shape[0])
        def _(r):
            out_ref[r] = feat_acc[r].astype(out_ref.dtype)


def hidden_call(down_index, up_index, grads, slope, w_down, w_up):
    feats, rows, side = grads.shape
    hids = slope.shape[0]
    count = w_down.shape[0]
    per_step = chunk_of(count, 24)
    group = chunk_of(per_step, 8)
    steps = count // per_step
    whole = lambda shape: pl.BlockSpec(shape, lambda p, s, *_: (0, 0, 0))
    return pl.pallas_call(
        functools.partial(hidden_kernel, per_step, group),
        grid_spec=pltpu.PrefetchScalarGridSpec(
            num_scalar_prefetch=2,
            grid=(2, steps),
            in_specs=[
                whole(grads.shape),
                whole(slope.shape),
                pl.BlockSpec(
                    (per_step, side, side),
                    lambda p, s, *_: (jnp.where(p == 0, s, steps - 1), 0, 0),
                ),
                pl.BlockSpec(
                    (per_step, side, side),
                    lambda p, s, *_: (jnp.where(p == 0, 0, s), 0, 0),
                ),
            ],
            out_specs=whole(grads.shape),
            scratch_shapes=[
                pltpu.VMEM((hids, rows, side), jnp.float32),
                pltpu.VMEM((hids, rows, side), jnp.bfloat16),
                pltpu.VMEM((feats, rows, side), jnp.float32),
            ],
        ),
        out_shape=jax.ShapeDtypeStruct(grads.shape, jnp.bfloat16),
        compiler_params=pltpu.CompilerParams(vmem_limit_bytes=VMEM_BYTES),
        cost_estimate=pl.CostEstimate(
            flops=4 * count * rows * side * side,
            bytes_accessed=4 * count * side * side,
            transcendentals=0,
        ),
        name="hidden_grads",
    )(down_index, up_index, grads, slope, w_down, w_up)


def item_place(chunks, t):
    half, r = t // (2 * chunks), t % (2 * chunks)
    c, low = r // 2, r % 2
    return jnp.where(low == 0, DEEP - 1 - half, half), c


def early_kernel(chunks, per, hid_ids, feat_ids, act_ref, grad_ref, out_ref):
    x = lax.axis_index("dp") % WIDE
    n = per // chunks

    @pl.loop(0, out_ref.shape[0])
    def _(t):
        zt, c = item_place(chunks, t)
        base = (zt * WIDE + 1 - x) * per + c * n
        for i in range(n):
            out_ref[t, i] = jnp.dot(
                act_ref[hid_ids[base + i]],
                grad_ref[feat_ids[base + i]],
                preferred_element_type=jnp.float32,
            ).astype(out_ref.dtype)


def weight_kernel(
    chunks, early, ahead, scale, hid_ids, feat_ids, act_ref, grad_ref, early_ref,
    out_ref, x_out, x_in, up_in, dn_in, z_out, acc,
    x_send, x_recv, up_recv, dn_recv, z_send,
):
    blk = lax.axis_index("blk")
    dp = lax.axis_index("dp")
    z, x = dp // WIDE, dp % WIDE
    per = out_ref.shape[0]
    n = per // chunks
    items = DEEP * chunks

    def at(zz, xx):
        return (zz * WIDE + xx, blk)

    barrier = pltpu.get_barrier_semaphore()
    pl.semaphore_signal(barrier, inc=1, device_id=at(z, 1 - x), device_id_type=MESH)

    @pl.when(z > 0)
    def _():
        pl.semaphore_signal(barrier, inc=1, device_id=at(z - 1, x), device_id_type=MESH)

    @pl.when(z < DEEP - 1)
    def _():
        pl.semaphore_signal(barrier, inc=1, device_id=at(z + 1, x), device_id_type=MESH)

    peers = 1 + (z > 0).astype(jnp.int32) + (z < DEEP - 1).astype(jnp.int32)
    pl.semaphore_wait(barrier, peers)

    def place(t):
        return item_place(chunks, t)

    def product(k):
        return jnp.dot(
            act_ref[hid_ids[k]], grad_ref[feat_ids[k]], preferred_element_type=jnp.float32
        )

    def x_copy(t):
        return pltpu.make_async_remote_copy(
            src_ref=x_out.at[t - early], dst_ref=x_in.at[t - early],
            send_sem=x_send.at[t - early], recv_sem=x_recv.at[t - early],
            device_id=at(z, 1 - x), device_id_type=MESH,
        )

    def up_copy(t):
        return pltpu.make_async_remote_copy(
            src_ref=z_out.at[t], dst_ref=up_in.at[t], send_sem=z_send.at[t],
            recv_sem=up_recv.at[t], device_id=at(z + 1, x), device_id_type=MESH,
        )

    def dn_copy(t):
        return pltpu.make_async_remote_copy(
            src_ref=z_out.at[t], dst_ref=dn_in.at[t], send_sem=z_send.at[t],
            recv_sem=dn_recv.at[t], device_id=at(z - 1, x), device_id_type=MESH,
        )

    def send_x(t):
        zt, c = place(t)
        base = (zt * WIDE + 1 - x) * per + c * n
        for i in range(n):
            x_out[t - early, i] = product(base + i).astype(x_out.dtype)
        x_copy(t).start()

    def handle(t):
        zt, c = place(t)
        base = (zt * WIDE + x) * per + c * n
        for i in range(n):
            acc[i] = product(base + i)

        @pl.when(t < early)
        def _():
            acc[...] += early_ref[jnp.minimum(t, early - 1)].astype(jnp.float32)

        @pl.when(t >= early)
        def _():
            x_copy(t).wait_recv()
            acc[...] += x_in[t - early].astype(jnp.float32)

        @pl.when((z <= zt) & (z > 0))
        def _():
            up_copy(t).wait_recv()
            acc[...] += up_in[t].astype(jnp.float32)

        @pl.when((z >= zt) & (z < DEEP - 1))
        def _():
            dn_copy(t).wait_recv()
            acc[...] += dn_in[t].astype(jnp.float32)

        @pl.when(z == zt)
        def _():
            out_ref[pl.ds(c * n, n)] = acc[...] * scale

        @pl.when(z < zt)
        def _():
            z_out[t] = acc[...].astype(z_out.dtype)
            up_copy(t).start()

        @pl.when(z > zt)
        def _():
            z_out[t] = acc[...].astype(z_out.dtype)
            dn_copy(t).start()

    @pl.loop(early, early + ahead)
    def _(t):
        send_x(t)

    @pl.loop(0, items + DEEP - 1)
    def _(u):
        later = early + ahead + u // 2 - 1

        @pl.when((u % 2 == 0) & (u > 0) & (later < items))
        def _():
            x_copy(later - ahead).wait_send()
            send_x(later)

        @pl.loop(0, DEEP)
        def _(lag):
            t = u - lag
            safe = jnp.clip(t, 0, items - 1)
            zt, _ = place(safe)
            late = jnp.where(
                z < zt, z, jnp.where(z > zt, DEEP - 1 - z, jnp.maximum(z, DEEP - 1 - z))
            )

            @pl.when((t >= 0) & (t < items) & (late == lag))
            def _():
                handle(safe)

    @pl.loop(items - ahead, items)
    def _(t):
        x_copy(t).wait_send()

    @pl.loop(0, items)
    def _(t):
        zt, _ = place(t)

        @pl.when(z != zt)
        def _():
            up_copy(t).wait_send()


def weight_call(hid_ids, feat_ids, acts, grads, scale):
    side, rows = acts.shape[1:]
    count = hid_ids.shape[0]
    per = count // (DEEP * WIDE)
    chunks = chunk_of(per, 6)
    n = per // chunks
    items = DEEP * chunks
    early = items * 3 // 8
    late = items - early
    ahead = late // 2
    smem, vmem = (pl.BlockSpec(memory_space=m) for m in (pltpu.SMEM, pltpu.VMEM))
    cost = lambda share: pl.CostEstimate(
        flops=2 * int(count * share) * rows * side * side,
        bytes_accessed=4 * count * side * side,
        transcendentals=0,
    )
    first = pl.pallas_call(
        functools.partial(early_kernel, chunks, per),
        out_shape=jax.ShapeDtypeStruct((early, n, side, side), jnp.bfloat16),
        in_specs=[smem] * 2 + [vmem] * 2,
        out_specs=vmem,
        compiler_params=pltpu.CompilerParams(vmem_limit_bytes=VMEM_BYTES),
        cost_estimate=cost(0.2),
        name="early_grads",
    )(hid_ids, feat_ids, acts, grads)
    first = lax.ppermute(first, "dp", [(d, d ^ 1) for d in range(DEEP * WIDE)])
    slot = lambda k: pltpu.VMEM((k, n, side, side), jnp.bfloat16)
    sems = lambda k: pltpu.SemaphoreType.DMA((k,))
    return pl.pallas_call(
        functools.partial(weight_kernel, chunks, early, ahead, scale),
        out_shape=jax.ShapeDtypeStruct((per, side, side), jnp.float32),
        in_specs=[smem] * 2 + [vmem] * 3,
        out_specs=vmem,
        scratch_shapes=[slot(late)] * 2
        + [slot(items)] * 3
        + [pltpu.VMEM((n, side, side), jnp.float32)]
        + [sems(late)] * 2
        + [sems(items)] * 3,
        compiler_params=pltpu.CompilerParams(
            collective_id=0, has_side_effects=True, vmem_limit_bytes=VMEM_BYTES
        ),
        cost_estimate=cost(0.8),
        name="weight_grads",
    )(hid_ids, feat_ids, acts, grads, first)


def gelu_parts(pre):
    normal_cdf = 0.5 * (1.0 + lax.erf(pre * inv_root_two))
    slope = normal_cdf + pre * jnp.exp(-0.5 * pre * pre) * inv_root_twopi
    return (pre * normal_cdf).astype(jnp.bfloat16), slope


def gather_kernel(
    parts, hid_ref, own_ref, grad_ref, slope_ref, act_ref,
    y_send, y_recv, c_send, c_recv, f_send, f_recv,
):
    dp, blk = lax.axis_index("dp"), lax.axis_index("blk")
    core, y = blk % 2, blk // 2
    beside, across = y * 2 + 1 - core, (1 - y) * 2 + core
    side = grad_ref.shape[2]
    feats = own_ref.shape[1] // side
    hids = act_ref.shape[0]
    n, h = feats // parts, hids // parts

    barrier = pltpu.get_barrier_semaphore()
    for peer in (beside, across):
        pl.semaphore_signal(barrier, inc=1, device_id=(dp, peer), device_id_type=MESH)
    for f in range(feats):
        grad_ref[blk * feats + f] = own_ref[:, f * side : (f + 1) * side]
    pl.semaphore_wait(barrier, 2)

    def copy(origin, q, target, send, recv):
        place = grad_ref.at[pl.ds(origin * feats + q * n, n)]
        return pltpu.make_async_remote_copy(
            src_ref=place, dst_ref=place, send_sem=send.at[q], recv_sem=recv.at[q],
            device_id=(dp, target), device_id_type=MESH,
        )

    for q in range(parts):
        copy(blk, q, across, y_send, y_recv).start()
    for q in range(parts):
        copy(blk, q, beside, c_send, c_recv).start()
    for q in range(parts):

        @pl.loop(q * h, (q + 1) * h)
        def _(c):
            pre = hid_ref[:, pl.ds(pl.multiple_of(c * side, side), side)]
            act, slope = gelu_parts(pre.astype(jnp.float32))
            slope_ref[c] = slope
            act_ref[c] = act.T

        copy(across, q, across, y_send, y_recv).wait_recv()
        copy(across, q, beside, f_send, f_recv).start()
    for q in range(parts):
        copy(blk, q, across, y_send, y_recv).wait_send()
        copy(blk, q, beside, c_send, c_recv).wait_send()
        copy(beside, q, beside, c_send, c_recv).wait_recv()
        copy(across, q, beside, f_send, f_recv).wait_send()
        copy(beside ^ 2, q, beside, f_send, f_recv).wait_recv()


def gather_call(hidden_pre, out_grad, side, feats):
    rows, hid_width = hidden_pre.shape
    hids = hid_width // side
    parts = next(n for n in (4, 2, 1) if feats // 4 % n == 0 and hids % n == 0)
    vmem = pl.BlockSpec(memory_space=pltpu.VMEM)
    return pl.pallas_call(
        functools.partial(gather_kernel, parts),
        out_shape=(
            jax.ShapeDtypeStruct((feats, rows, side), jnp.bfloat16),
            jax.ShapeDtypeStruct((hids, rows, side), jnp.float32),
            jax.ShapeDtypeStruct((hids, side, rows), jnp.bfloat16),
        ),
        in_specs=[vmem] * 2,
        out_specs=(vmem,) * 3,
        scratch_shapes=[pltpu.SemaphoreType.DMA((parts,))] * 6,
        compiler_params=pltpu.CompilerParams(
            collective_id=1, has_side_effects=True, vmem_limit_bytes=VMEM_BYTES
        ),
        cost_estimate=pl.CostEstimate(
            flops=40 * rows * hid_width,
            bytes_accessed=8 * rows * hid_width,
            transcendentals=2 * rows * hid_width,
        ),
        name="gather_gelu",
    )(hidden_pre, out_grad)


def local(hidden_pre, out_grad, w_up_blocks, up_index, w_down_blocks, down_index):
    rows, hid_width = hidden_pre.shape
    side = w_up_blocks.shape[1]
    hids = hid_width // side
    count = w_down_blocks.shape[0]
    dp_size = lax.axis_size("dp")
    scale = float((rows * dp_size) ** (-0.5))
    if lax.axis_size("blk") == 4:
        feats = 4 * out_grad.shape[1] // side
        grads, slope, acts = gather_call(hidden_pre, out_grad, side, feats)
    else:
        own = out_grad.reshape(rows, -1, side).transpose(1, 0, 2)
        grads = lax.all_gather(own, "blk", axis=0, tiled=True)
        acts, slope = gelu_parts(hidden_pre.astype(jnp.float32))
        slope = slope.reshape(rows, hids, side).transpose(1, 0, 2)
        acts = acts.reshape(rows, hids, side).transpose(1, 2, 0)
    partial_sum = hidden_call(down_index, up_index, grads, slope, w_down_blocks, w_up_blocks)
    summed = lax.psum_scatter(partial_sum, "blk", scatter_dimension=0, tiled=True)
    summed = summed.transpose(1, 0, 2).reshape(rows, -1)
    if dp_size == DEEP * WIDE and count % dp_size == 0:
        weight_out = weight_call(down_index[:, 1], down_index[:, 0], acts, grads, scale)
        weight_out = weight_out.reshape(-1, side)
    else:
        local_grad = jnp.einsum(
            "bit,btj->bij",
            jnp.take(acts, down_index[:, 1], axis=0),
            jnp.take(grads, down_index[:, 0], axis=0),
            preferred_element_type=jnp.float32,
        )
        weight_out = lax.psum_scatter(
            (local_grad * scale).reshape(-1, side), "dp", scatter_dimension=0, tiled=True
        )
    return (summed, weight_out)


def solution(mesh):
    placed = (
        P("dp", "blk"),
        P("dp", "blk"),
        P("blk", None, None),
        P("blk", None),
        P("blk", None, None),
        P("blk", None),
    )
    return jax.shard_map(
        local,
        mesh=mesh,
        in_specs=placed,
        out_specs=(P("dp", "blk"), P(("blk", "dp"), None)),
        check_vma=False,
    )
```

```python
import functools

import jax
import jax.numpy as jnp
from jax import lax
from jax.experimental import pallas as pl
from jax.experimental.pallas import tpu as pltpu
from jax.sharding import PartitionSpec as P

inv_root_two = 0.7071067811865476
inv_root_twopi = 0.3989422804014327
MESH = pl.DeviceIdType.MESH
VMEM_BYTES = 58 << 20
DEEP, WIDE = 4, 2


def contract_last(a, b):
    return lax.dot_general(
        a, b, (((1,), (1,)), ((), ())), preferred_element_type=jnp.float32
    )


def chunk_of(count, most):
    return max(n for n in range(1, most + 1) if count % n == 0)


def hidden_kernel(
    per_step, group, down_ref, up_ref, grad_ref, slope_ref, wd_ref, wu_ref, out_ref,
    hid_acc, pre, feat_acc,
):
    phase, step = pl.program_id(0), pl.program_id(1)
    last = pl.num_programs(1) - 1

    @pl.when((phase == 0) & (step == 0))
    def _():
        hid_acc[...] = jnp.zeros_like(hid_acc)
        feat_acc[...] = jnp.zeros_like(feat_acc)

    @pl.when(phase == 0)
    def _():
        @pl.loop(0, per_step // group)
        def _(g):
            first = step * per_step + g * group
            for i in range(group):
                hid_acc[down_ref[first + i, 1]] += contract_last(
                    grad_ref[down_ref[first + i, 0]], wd_ref[g * group + i]
                )

    @pl.when((phase == 0) & (step == last))
    def _():
        @pl.loop(0, pre.shape[0])
        def _(c):
            pre[c] = (hid_acc[c] * slope_ref[c]).astype(pre.dtype)

    @pl.when(phase == 1)
    def _():
        @pl.loop(0, per_step // group)
        def _(g):
            first = step * per_step + g * group
            for i in range(group):
                feat_acc[up_ref[first + i, 0]] += contract_last(
                    pre[up_ref[first + i, 1]], wu_ref[g * group + i]
                )

    @pl.when((phase == 1) & (step == last))
    def _():
        @pl.loop(0, feat_acc.shape[0])
        def _(r):
            out_ref[r] = feat_acc[r].astype(out_ref.dtype)


def hidden_call(down_index, up_index, grads, slope, w_down, w_up):
    feats, rows, side = grads.shape
    hids = slope.shape[0]
    count = w_down.shape[0]
    per_step = chunk_of(count, 24)
    group = chunk_of(per_step, 12)
    steps = count // per_step
    whole = lambda shape: pl.BlockSpec(shape, lambda p, s, *_: (0, 0, 0))
    return pl.pallas_call(
        functools.partial(hidden_kernel, per_step, group),
        grid_spec=pltpu.PrefetchScalarGridSpec(
            num_scalar_prefetch=2,
            grid=(2, steps),
            in_specs=[
                whole(grads.shape),
                whole(slope.shape),
                pl.BlockSpec(
                    (per_step, side, side),
                    lambda p, s, *_: (jnp.where(p == 0, s, steps - 1), 0, 0),
                ),
                pl.BlockSpec(
                    (per_step, side, side),
                    lambda p, s, *_: (jnp.where(p == 0, 0, s), 0, 0),
                ),
            ],
            out_specs=whole(grads.shape),
            scratch_shapes=[
                pltpu.VMEM((hids, rows, side), jnp.float32),
                pltpu.VMEM((hids, rows, side), jnp.bfloat16),
                pltpu.VMEM((feats, rows, side), jnp.float32),
            ],
        ),
        out_shape=jax.ShapeDtypeStruct(grads.shape, jnp.bfloat16),
        compiler_params=pltpu.CompilerParams(vmem_limit_bytes=VMEM_BYTES),
        cost_estimate=pl.CostEstimate(
            flops=4 * count * rows * side * side,
            bytes_accessed=4 * count * side * side,
            transcendentals=0,
        ),
        name="hidden_grads",
    )(down_index, up_index, grads, slope, w_down, w_up)


def weight_kernel(
    chunks, ahead, scale, hid_ids, feat_ids, act_ref, grad_ref, out_ref,
    x_out, x_in, up_in, dn_in, z_out, acc,
    x_send, x_recv, up_recv, dn_recv, z_send,
):
    blk = lax.axis_index("blk")
    dp = lax.axis_index("dp")
    z, x = dp // WIDE, dp % WIDE
    per = out_ref.shape[0]
    n = per // chunks
    items = DEEP * chunks

    def at(zz, xx):
        return (zz * WIDE + xx, blk)

    barrier = pltpu.get_barrier_semaphore()
    pl.semaphore_signal(barrier, inc=1, device_id=at(z, 1 - x), device_id_type=MESH)

    @pl.when(z > 0)
    def _():
        pl.semaphore_signal(barrier, inc=1, device_id=at(z - 1, x), device_id_type=MESH)

    @pl.when(z < DEEP - 1)
    def _():
        pl.semaphore_signal(barrier, inc=1, device_id=at(z + 1, x), device_id_type=MESH)

    peers = 1 + (z > 0).astype(jnp.int32) + (z < DEEP - 1).astype(jnp.int32)
    pl.semaphore_wait(barrier, peers)

    def place(t):
        half, r = t // (2 * chunks), t % (2 * chunks)
        c, low = r // 2, r % 2
        return jnp.where(low == 0, DEEP - 1 - half, half), c

    def product(k):
        return jnp.dot(
            act_ref[hid_ids[k]], grad_ref[feat_ids[k]], preferred_element_type=jnp.float32
        )

    def x_copy(t):
        return pltpu.make_async_remote_copy(
            src_ref=x_out.at[t], dst_ref=x_in.at[t], send_sem=x_send.at[t],
            recv_sem=x_recv.at[t], device_id=at(z, 1 - x), device_id_type=MESH,
        )

    def up_copy(t):
        return pltpu.make_async_remote_copy(
            src_ref=z_out.at[t], dst_ref=up_in.at[t], send_sem=z_send.at[t],
            recv_sem=up_recv.at[t], device_id=at(z + 1, x), device_id_type=MESH,
        )

    def dn_copy(t):
        return pltpu.make_async_remote_copy(
            src_ref=z_out.at[t], dst_ref=dn_in.at[t], send_sem=z_send.at[t],
            recv_sem=dn_recv.at[t], device_id=at(z - 1, x), device_id_type=MESH,
        )

    def send_x(t):
        zt, c = place(t)
        base = (zt * WIDE + 1 - x) * per + c * n
        for i in range(n):
            x_out[t, i] = product(base + i).astype(x_out.dtype)
        x_copy(t).start()

    def handle(t):
        zt, c = place(t)
        base = (zt * WIDE + x) * per + c * n
        for i in range(n):
            acc[i] = product(base + i)
        x_copy(t).wait_recv()
        acc[...] += x_in[t].astype(jnp.float32)

        @pl.when((z <= zt) & (z > 0))
        def _():
            up_copy(t).wait_recv()
            acc[...] += up_in[t].astype(jnp.float32)

        @pl.when((z >= zt) & (z < DEEP - 1))
        def _():
            dn_copy(t).wait_recv()
            acc[...] += dn_in[t].astype(jnp.float32)

        @pl.when(z == zt)
        def _():
            out_ref[pl.ds(c * n, n)] = acc[...] * scale

        @pl.when(z < zt)
        def _():
            z_out[t] = acc[...].astype(z_out.dtype)
            up_copy(t).start()

        @pl.when(z > zt)
        def _():
            z_out[t] = acc[...].astype(z_out.dtype)
            dn_copy(t).start()

    @pl.loop(0, ahead)
    def _(t):
        send_x(t)

    @pl.loop(0, items + DEEP - 1)
    def _(u):
        @pl.when(u + ahead < items)
        def _():
            x_copy(u).wait_send()
            send_x(u + ahead)

        @pl.loop(0, DEEP)
        def _(lag):
            t = u - lag
            safe = jnp.clip(t, 0, items - 1)
            zt, _ = place(safe)
            late = jnp.where(
                z < zt, z, jnp.where(z > zt, DEEP - 1 - z, jnp.maximum(z, DEEP - 1 - z))
            )

            @pl.when((t >= 0) & (t < items) & (late == lag))
            def _():
                handle(safe)

    @pl.loop(items - ahead, items)
    def _(t):
        x_copy(t).wait_send()

    @pl.loop(0, items)
    def _(t):
        zt, _ = place(t)

        @pl.when(z != zt)
        def _():
            up_copy(t).wait_send()


def weight_call(hid_ids, feat_ids, acts, grads, scale):
    hids, side, rows = acts.shape
    count = hid_ids.shape[0]
    per = count // (DEEP * WIDE)
    chunks = chunk_of(per, 6)
    n = per // chunks
    items = DEEP * chunks
    ahead = min(5, items)
    slots = pltpu.VMEM((items, n, side, side), jnp.bfloat16)
    sems = pltpu.SemaphoreType.DMA((items,))
    return pl.pallas_call(
        functools.partial(weight_kernel, chunks, ahead, scale),
        out_shape=jax.ShapeDtypeStruct((per, side, side), jnp.float32),
        in_specs=[pl.BlockSpec(memory_space=pltpu.SMEM)] * 2
        + [pl.BlockSpec(memory_space=pltpu.VMEM)] * 2,
        out_specs=pl.BlockSpec(memory_space=pltpu.VMEM),
        scratch_shapes=[slots] * 5
        + [pltpu.VMEM((n, side, side), jnp.float32)]
        + [sems] * 5,
        compiler_params=pltpu.CompilerParams(
            collective_id=0, has_side_effects=True, vmem_limit_bytes=VMEM_BYTES
        ),
        cost_estimate=pl.CostEstimate(
            flops=2 * count * rows * side * side,
            bytes_accessed=4 * count * side * side,
            transcendentals=0,
        ),
        name="weight_grads",
    )(hid_ids, feat_ids, acts, grads)


def gelu_parts(pre):
    normal_cdf = 0.5 * (1.0 + lax.erf(pre * inv_root_two))
    slope = normal_cdf + pre * jnp.exp(-0.5 * pre * pre) * inv_root_twopi
    return (pre * normal_cdf).astype(jnp.bfloat16), slope


def gather_kernel(
    parts, hid_ref, own_ref, grad_ref, slope_ref, act_ref,
    y_send, y_recv, c_send, c_recv, f_send, f_recv,
):
    dp, blk = lax.axis_index("dp"), lax.axis_index("blk")
    core, y = blk % 2, blk // 2
    beside, across = y * 2 + 1 - core, (1 - y) * 2 + core
    side = grad_ref.shape[2]
    feats = own_ref.shape[1] // side
    hids = act_ref.shape[0]
    n, h = feats // parts, hids // parts

    barrier = pltpu.get_barrier_semaphore()
    for peer in (beside, across):
        pl.semaphore_signal(barrier, inc=1, device_id=(dp, peer), device_id_type=MESH)
    for f in range(feats):
        grad_ref[blk * feats + f] = own_ref[:, f * side : (f + 1) * side]
    pl.semaphore_wait(barrier, 2)

    def copy(origin, q, target, send, recv):
        place = grad_ref.at[pl.ds(origin * feats + q * n, n)]
        return pltpu.make_async_remote_copy(
            src_ref=place, dst_ref=place, send_sem=send.at[q], recv_sem=recv.at[q],
            device_id=(dp, target), device_id_type=MESH,
        )

    for q in range(parts):
        copy(blk, q, across, y_send, y_recv).start()
    for q in range(parts):
        copy(blk, q, beside, c_send, c_recv).start()
    for q in range(parts):

        @pl.loop(q * h, (q + 1) * h)
        def _(c):
            pre = hid_ref[:, pl.ds(pl.multiple_of(c * side, side), side)]
            act, slope = gelu_parts(pre.astype(jnp.float32))
            slope_ref[c] = slope
            act_ref[c] = act.T

        copy(across, q, across, y_send, y_recv).wait_recv()
        copy(across, q, beside, f_send, f_recv).start()
    for q in range(parts):
        copy(blk, q, across, y_send, y_recv).wait_send()
        copy(blk, q, beside, c_send, c_recv).wait_send()
        copy(beside, q, beside, c_send, c_recv).wait_recv()
        copy(across, q, beside, f_send, f_recv).wait_send()
        copy(beside ^ 2, q, beside, f_send, f_recv).wait_recv()


def gather_call(hidden_pre, out_grad, side, feats):
    rows, hid_width = hidden_pre.shape
    hids = hid_width // side
    parts = next(n for n in (4, 2, 1) if feats // 4 % n == 0 and hids % n == 0)
    vmem = pl.BlockSpec(memory_space=pltpu.VMEM)
    return pl.pallas_call(
        functools.partial(gather_kernel, parts),
        out_shape=(
            jax.ShapeDtypeStruct((feats, rows, side), jnp.bfloat16),
            jax.ShapeDtypeStruct((hids, rows, side), jnp.float32),
            jax.ShapeDtypeStruct((hids, side, rows), jnp.bfloat16),
        ),
        in_specs=[vmem] * 2,
        out_specs=(vmem,) * 3,
        scratch_shapes=[pltpu.SemaphoreType.DMA((parts,))] * 6,
        compiler_params=pltpu.CompilerParams(
            collective_id=1, has_side_effects=True, vmem_limit_bytes=VMEM_BYTES
        ),
        cost_estimate=pl.CostEstimate(
            flops=40 * rows * hid_width,
            bytes_accessed=8 * rows * hid_width,
            transcendentals=2 * rows * hid_width,
        ),
        name="gather_gelu",
    )(hidden_pre, out_grad)


def local(hidden_pre, out_grad, w_up_blocks, up_index, w_down_blocks, down_index):
    rows, hid_width = hidden_pre.shape
    side = w_up_blocks.shape[1]
    hids = hid_width // side
    count = w_down_blocks.shape[0]
    dp_size = lax.axis_size("dp")
    scale = float((rows * dp_size) ** (-0.5))
    if lax.axis_size("blk") == 4:
        feats = 4 * out_grad.shape[1] // side
        grads, slope, acts = gather_call(hidden_pre, out_grad, side, feats)
    else:
        own = out_grad.reshape(rows, -1, side).transpose(1, 0, 2)
        grads = lax.all_gather(own, "blk", axis=0, tiled=True)
        acts, slope = gelu_parts(hidden_pre.astype(jnp.float32))
        slope = slope.reshape(rows, hids, side).transpose(1, 0, 2)
        acts = acts.reshape(rows, hids, side).transpose(1, 2, 0)
    partial_sum = hidden_call(down_index, up_index, grads, slope, w_down_blocks, w_up_blocks)
    summed = lax.psum_scatter(partial_sum, "blk", scatter_dimension=0, tiled=True)
    summed = summed.transpose(1, 0, 2).reshape(rows, -1)
    if dp_size == DEEP * WIDE and count % dp_size == 0:
        weight_out = weight_call(down_index[:, 1], down_index[:, 0], acts, grads, scale)
        weight_out = weight_out.reshape(-1, side)
    else:
        local_grad = jnp.einsum(
            "bit,btj->bij",
            jnp.take(acts, down_index[:, 1], axis=0),
            jnp.take(grads, down_index[:, 0], axis=0),
            preferred_element_type=jnp.float32,
        )
        weight_out = lax.psum_scatter(
            (local_grad * scale).reshape(-1, side), "dp", scatter_dimension=0, tiled=True
        )
    return (summed, weight_out)


def solution(mesh):
    placed = (
        P("dp", "blk"),
        P("dp", "blk"),
        P("blk", None, None),
        P("blk", None),
        P("blk", None, None),
        P("blk", None),
    )
    return jax.shard_map(
        local,
        mesh=mesh,
        in_specs=placed,
        out_specs=(P("dp", "blk"), P(("blk", "dp"), None)),
        check_vma=False,
    )
```

```python
import functools

import jax
import jax.numpy as jnp
from jax import lax
from jax.experimental import pallas as pl
from jax.experimental.pallas import tpu as pltpu
from jax.sharding import PartitionSpec as P

inv_root_two = 0.7071067811865476
inv_root_twopi = 0.3989422804014327
MESH = pl.DeviceIdType.MESH
VMEM_BYTES = 58 << 20
DEEP, WIDE = 4, 2


def contract_last(a, b):
    return lax.dot_general(
        a, b, (((1,), (1,)), ((), ())), preferred_element_type=jnp.float32
    )


def chunk_of(count, most):
    return max(n for n in range(1, most + 1) if count % n == 0)


def hidden_kernel(
    per_step, group, down_ref, up_ref, grad_ref, slope_ref, wd_ref, wu_ref, out_ref,
    hid_acc, pre, feat_acc,
):
    phase, step = pl.program_id(0), pl.program_id(1)
    last = pl.num_programs(1) - 1

    @pl.when((phase == 0) & (step == 0))
    def _():
        hid_acc[...] = jnp.zeros_like(hid_acc)
        feat_acc[...] = jnp.zeros_like(feat_acc)

    @pl.when(phase == 0)
    def _():
        @pl.loop(0, per_step // group)
        def _(g):
            first = step * per_step + g * group
            for i in range(group):
                hid_acc[down_ref[first + i, 1]] += contract_last(
                    grad_ref[down_ref[first + i, 0]], wd_ref[g * group + i]
                )

    @pl.when((phase == 0) & (step == last))
    def _():
        @pl.loop(0, pre.shape[0])
        def _(c):
            pre[c] = (hid_acc[c] * slope_ref[c]).astype(pre.dtype)

    @pl.when(phase == 1)
    def _():
        @pl.loop(0, per_step // group)
        def _(g):
            first = step * per_step + g * group
            for i in range(group):
                feat_acc[up_ref[first + i, 0]] += contract_last(
                    pre[up_ref[first + i, 1]], wu_ref[g * group + i]
                )

    @pl.when((phase == 1) & (step == last))
    def _():
        @pl.loop(0, feat_acc.shape[0])
        def _(r):
            out_ref[r] = feat_acc[r].astype(out_ref.dtype)


def hidden_call(down_index, up_index, grads, slope, w_down, w_up):
    feats, rows, side = grads.shape
    hids = slope.shape[0]
    count = w_down.shape[0]
    per_step = chunk_of(count, 24)
    group = chunk_of(per_step, 12)
    steps = count // per_step
    whole = lambda shape: pl.BlockSpec(shape, lambda p, s, *_: (0, 0, 0))
    return pl.pallas_call(
        functools.partial(hidden_kernel, per_step, group),
        grid_spec=pltpu.PrefetchScalarGridSpec(
            num_scalar_prefetch=2,
            grid=(2, steps),
            in_specs=[
                whole(grads.shape),
                whole(slope.shape),
                pl.BlockSpec(
                    (per_step, side, side),
                    lambda p, s, *_: (jnp.where(p == 0, s, steps - 1), 0, 0),
                ),
                pl.BlockSpec(
                    (per_step, side, side),
                    lambda p, s, *_: (jnp.where(p == 0, 0, s), 0, 0),
                ),
            ],
            out_specs=whole(grads.shape),
            scratch_shapes=[
                pltpu.VMEM((hids, rows, side), jnp.float32),
                pltpu.VMEM((hids, rows, side), jnp.bfloat16),
                pltpu.VMEM((feats, rows, side), jnp.float32),
            ],
        ),
        out_shape=jax.ShapeDtypeStruct(grads.shape, jnp.bfloat16),
        compiler_params=pltpu.CompilerParams(vmem_limit_bytes=VMEM_BYTES),
        cost_estimate=pl.CostEstimate(
            flops=4 * count * rows * side * side,
            bytes_accessed=4 * count * side * side,
            transcendentals=0,
        ),
        name="hidden_grads",
    )(down_index, up_index, grads, slope, w_down, w_up)


def weight_kernel(
    chunks, ahead, scale, hid_ids, feat_ids, act_ref, grad_ref, out_ref,
    x_out, x_in, up_in, dn_in, z_out, acc,
    x_send, x_recv, up_recv, dn_recv, z_send,
):
    blk = lax.axis_index("blk")
    dp = lax.axis_index("dp")
    z, x = dp // WIDE, dp % WIDE
    per = out_ref.shape[0]
    n = per // chunks
    items = DEEP * chunks

    def at(zz, xx):
        return (zz * WIDE + xx, blk)

    barrier = pltpu.get_barrier_semaphore()
    pl.semaphore_signal(barrier, inc=1, device_id=at(z, 1 - x), device_id_type=MESH)

    @pl.when(z > 0)
    def _():
        pl.semaphore_signal(barrier, inc=1, device_id=at(z - 1, x), device_id_type=MESH)

    @pl.when(z < DEEP - 1)
    def _():
        pl.semaphore_signal(barrier, inc=1, device_id=at(z + 1, x), device_id_type=MESH)

    peers = 1 + (z > 0).astype(jnp.int32) + (z < DEEP - 1).astype(jnp.int32)
    pl.semaphore_wait(barrier, peers)

    def place(t):
        half, r = t // (2 * chunks), t % (2 * chunks)
        c, low = r // 2, r % 2
        return jnp.where(low == 0, DEEP - 1 - half, half), c

    def product(k):
        return jnp.dot(
            act_ref[hid_ids[k]], grad_ref[feat_ids[k]], preferred_element_type=jnp.float32
        )

    def x_copy(t):
        return pltpu.make_async_remote_copy(
            src_ref=x_out.at[t], dst_ref=x_in.at[t], send_sem=x_send.at[t],
            recv_sem=x_recv.at[t], device_id=at(z, 1 - x), device_id_type=MESH,
        )

    def up_copy(t):
        return pltpu.make_async_remote_copy(
            src_ref=z_out.at[t], dst_ref=up_in.at[t], send_sem=z_send.at[t],
            recv_sem=up_recv.at[t], device_id=at(z + 1, x), device_id_type=MESH,
        )

    def dn_copy(t):
        return pltpu.make_async_remote_copy(
            src_ref=z_out.at[t], dst_ref=dn_in.at[t], send_sem=z_send.at[t],
            recv_sem=dn_recv.at[t], device_id=at(z - 1, x), device_id_type=MESH,
        )

    def send_x(t):
        zt, c = place(t)
        base = (zt * WIDE + 1 - x) * per + c * n
        for i in range(n):
            x_out[t, i] = product(base + i).astype(x_out.dtype)
        x_copy(t).start()

    def handle(t):
        zt, c = place(t)
        base = (zt * WIDE + x) * per + c * n
        for i in range(n):
            acc[i] = product(base + i)
        x_copy(t).wait_recv()
        acc[...] += x_in[t].astype(jnp.float32)

        @pl.when((z <= zt) & (z > 0))
        def _():
            up_copy(t).wait_recv()
            acc[...] += up_in[t].astype(jnp.float32)

        @pl.when((z >= zt) & (z < DEEP - 1))
        def _():
            dn_copy(t).wait_recv()
            acc[...] += dn_in[t].astype(jnp.float32)

        @pl.when(z == zt)
        def _():
            out_ref[pl.ds(c * n, n)] = acc[...] * scale

        @pl.when(z < zt)
        def _():
            z_out[t] = acc[...].astype(z_out.dtype)
            up_copy(t).start()

        @pl.when(z > zt)
        def _():
            z_out[t] = acc[...].astype(z_out.dtype)
            dn_copy(t).start()

    @pl.loop(0, ahead)
    def _(t):
        send_x(t)

    @pl.loop(0, items + DEEP - 1)
    def _(u):
        @pl.when(u + ahead < items)
        def _():
            x_copy(u).wait_send()
            send_x(u + ahead)

        @pl.loop(0, DEEP)
        def _(lag):
            t = u - lag
            safe = jnp.clip(t, 0, items - 1)
            zt, _ = place(safe)
            late = jnp.where(
                z < zt, z, jnp.where(z > zt, DEEP - 1 - z, jnp.maximum(z, DEEP - 1 - z))
            )

            @pl.when((t >= 0) & (t < items) & (late == lag))
            def _():
                handle(safe)

    @pl.loop(items - ahead, items)
    def _(t):
        x_copy(t).wait_send()

    @pl.loop(0, items)
    def _(t):
        zt, _ = place(t)

        @pl.when(z != zt)
        def _():
            up_copy(t).wait_send()


def weight_call(hid_ids, feat_ids, acts, grads, scale):
    hids, side, rows = acts.shape
    count = hid_ids.shape[0]
    per = count // (DEEP * WIDE)
    chunks = chunk_of(per, 9)
    n = per // chunks
    items = DEEP * chunks
    ahead = min(8, items)
    slots = pltpu.VMEM((items, n, side, side), jnp.bfloat16)
    sems = pltpu.SemaphoreType.DMA((items,))
    return pl.pallas_call(
        functools.partial(weight_kernel, chunks, ahead, scale),
        out_shape=jax.ShapeDtypeStruct((per, side, side), jnp.float32),
        in_specs=[pl.BlockSpec(memory_space=pltpu.SMEM)] * 2
        + [pl.BlockSpec(memory_space=pltpu.VMEM)] * 2,
        out_specs=pl.BlockSpec(memory_space=pltpu.VMEM),
        scratch_shapes=[slots] * 5
        + [pltpu.VMEM((n, side, side), jnp.float32)]
        + [sems] * 5,
        compiler_params=pltpu.CompilerParams(
            collective_id=0, has_side_effects=True, vmem_limit_bytes=VMEM_BYTES
        ),
        cost_estimate=pl.CostEstimate(
            flops=2 * count * rows * side * side,
            bytes_accessed=4 * count * side * side,
            transcendentals=0,
        ),
        name="weight_grads",
    )(hid_ids, feat_ids, acts, grads)


def gelu_parts(pre):
    normal_cdf = 0.5 * (1.0 + lax.erf(pre * inv_root_two))
    slope = normal_cdf + pre * jnp.exp(-0.5 * pre * pre) * inv_root_twopi
    return (pre * normal_cdf).astype(jnp.bfloat16), slope


def gather_kernel(
    parts, hid_ref, own_ref, grad_ref, slope_ref, act_ref,
    y_send, y_recv, c_send, c_recv, f_send, f_recv,
):
    dp, blk = lax.axis_index("dp"), lax.axis_index("blk")
    core, y = blk % 2, blk // 2
    beside, across = y * 2 + 1 - core, (1 - y) * 2 + core
    side = grad_ref.shape[2]
    feats = own_ref.shape[1] // side
    hids = act_ref.shape[0]
    n, h = feats // parts, hids // parts

    barrier = pltpu.get_barrier_semaphore()
    for peer in (beside, across):
        pl.semaphore_signal(barrier, inc=1, device_id=(dp, peer), device_id_type=MESH)
    for f in range(feats):
        grad_ref[blk * feats + f] = own_ref[:, f * side : (f + 1) * side]
    pl.semaphore_wait(barrier, 2)

    def copy(origin, q, target, send, recv):
        place = grad_ref.at[pl.ds(origin * feats + q * n, n)]
        return pltpu.make_async_remote_copy(
            src_ref=place, dst_ref=place, send_sem=send.at[q], recv_sem=recv.at[q],
            device_id=(dp, target), device_id_type=MESH,
        )

    for q in range(parts):
        copy(blk, q, across, y_send, y_recv).start()
    for q in range(parts):
        copy(blk, q, beside, c_send, c_recv).start()
    for q in range(parts):

        @pl.loop(q * h, (q + 1) * h)
        def _(c):
            pre = hid_ref[:, pl.ds(pl.multiple_of(c * side, side), side)]
            act, slope = gelu_parts(pre.astype(jnp.float32))
            slope_ref[c] = slope
            act_ref[c] = act.T

        copy(across, q, across, y_send, y_recv).wait_recv()
        copy(across, q, beside, f_send, f_recv).start()
    for q in range(parts):
        copy(blk, q, across, y_send, y_recv).wait_send()
        copy(blk, q, beside, c_send, c_recv).wait_send()
        copy(beside, q, beside, c_send, c_recv).wait_recv()
        copy(across, q, beside, f_send, f_recv).wait_send()
        copy(beside ^ 2, q, beside, f_send, f_recv).wait_recv()


def gather_call(hidden_pre, out_grad, side, feats):
    rows, hid_width = hidden_pre.shape
    hids = hid_width // side
    parts = next(n for n in (4, 2, 1) if feats // 4 % n == 0 and hids % n == 0)
    vmem = pl.BlockSpec(memory_space=pltpu.VMEM)
    return pl.pallas_call(
        functools.partial(gather_kernel, parts),
        out_shape=(
            jax.ShapeDtypeStruct((feats, rows, side), jnp.bfloat16),
            jax.ShapeDtypeStruct((hids, rows, side), jnp.float32),
            jax.ShapeDtypeStruct((hids, side, rows), jnp.bfloat16),
        ),
        in_specs=[vmem] * 2,
        out_specs=(vmem,) * 3,
        scratch_shapes=[pltpu.SemaphoreType.DMA((parts,))] * 6,
        compiler_params=pltpu.CompilerParams(
            collective_id=1, has_side_effects=True, vmem_limit_bytes=VMEM_BYTES
        ),
        cost_estimate=pl.CostEstimate(
            flops=40 * rows * hid_width,
            bytes_accessed=8 * rows * hid_width,
            transcendentals=2 * rows * hid_width,
        ),
        name="gather_gelu",
    )(hidden_pre, out_grad)


def local(hidden_pre, out_grad, w_up_blocks, up_index, w_down_blocks, down_index):
    rows, hid_width = hidden_pre.shape
    side = w_up_blocks.shape[1]
    hids = hid_width // side
    count = w_down_blocks.shape[0]
    dp_size = lax.axis_size("dp")
    scale = float((rows * dp_size) ** (-0.5))
    if lax.axis_size("blk") == 4:
        feats = 4 * out_grad.shape[1] // side
        grads, slope, acts = gather_call(hidden_pre, out_grad, side, feats)
    else:
        own = out_grad.reshape(rows, -1, side).transpose(1, 0, 2)
        grads = lax.all_gather(own, "blk", axis=0, tiled=True)
        acts, slope = gelu_parts(hidden_pre.astype(jnp.float32))
        slope = slope.reshape(rows, hids, side).transpose(1, 0, 2)
        acts = acts.reshape(rows, hids, side).transpose(1, 2, 0)
    partial_sum = hidden_call(down_index, up_index, grads, slope, w_down_blocks, w_up_blocks)
    summed = lax.psum_scatter(partial_sum, "blk", scatter_dimension=0, tiled=True)
    summed = summed.transpose(1, 0, 2).reshape(rows, -1)
    if dp_size == DEEP * WIDE and count % dp_size == 0:
        weight_out = weight_call(down_index[:, 1], down_index[:, 0], acts, grads, scale)
        weight_out = weight_out.reshape(-1, side)
    else:
        local_grad = jnp.einsum(
            "bit,btj->bij",
            jnp.take(acts, down_index[:, 1], axis=0),
            jnp.take(grads, down_index[:, 0], axis=0),
            preferred_element_type=jnp.float32,
        )
        weight_out = lax.psum_scatter(
            (local_grad * scale).reshape(-1, side), "dp", scatter_dimension=0, tiled=True
        )
    return (summed, weight_out)


def solution(mesh):
    placed = (
        P("dp", "blk"),
        P("dp", "blk"),
        P("blk", None, None),
        P("blk", None),
        P("blk", None, None),
        P("blk", None),
    )
    return jax.shard_map(
        local,
        mesh=mesh,
        in_specs=placed,
        out_specs=(P("dp", "blk"), P(("blk", "dp"), None)),
        check_vma=False,
    )
```
